128 devices in a mesh: samp: 8 (over y, core), snp: 16 (over z, x).
Axes of the slice: x: 4, y: 4, z: 4, core: 2. Of those that a mesh axis runs over, the one named last changes fastest.
Arguments:
- genotypes: int32 [24576, 22528], P('samp', 'snp'), may hold values from 0 to 2, as said below
- allele_counts: int32 [22528], P('snp'), may hold values from 2 to 49150, as said below
- ridge_delta: float32 [4], replicated, may hold values from 0.3 to 3
- solution: float32 [4, 24576], P(None, ('samp', 'snp')), may hold values from -6 to 6
- residual: float32 [4, 24576], P(None, ('samp', 'snp')), may hold values from -6 to 6
- direction: float32 [4, 24576], P(None, ('samp', 'snp')), may hold values from -6 to 6
Outputs:
- solution_out: float32 [4, 24576], P(None, ('samp', 'snp'))
- residual_out: float32 [4, 24576], P(None, ('samp', 'snp'))
- direction_out: float32 [4, 24576], P(None, ('samp', 'snp'))
The draws below stay inside these ranges and needn't reach their ends.
Inputs may be any that keep to these rules, and one draw needn't show every extreme that they name: `genotypes`: every SNP has at least one sample of dosage 0 and at least one of dosage 2. allele_counts[j] is the sum of genotypes[:, j] over all 24576 samples.
All inputs are finite; a program needn't handle non-finite values.
Results may differ from the reference program's by a relative error of at most 0.0003.
Values sent between devices are 32-bit elements; how exact they have to be, the bound alone decides.
No kernel may reach another device: no remote copies, remote signals or barrier semaphores. Data moves between devices by JAX's collectives and lax.ppermute only.
A program may use at most 128 MiB of HBM per device.

```python
import math
import jax
import jax.numpy as jnp
from jax import lax

SNP_DEV = 1408
RHS = 4
ITERS = 3
SAMPLES = 24576
SNPS = 22528
N_SNP = 16


def dosage_matrix(key):
    base_key = jax.random.fold_in(key, 11)
    key_freq, key_draw, key_low, key_high = jax.random.split(base_key, 4)
    thresholds = jax.random.randint(key_freq, (1, SNPS), 3277, 29492, dtype=jnp.int32)
    raw_bits = jax.random.randint(key_draw, (SAMPLES, SNPS), 0, 1 << 30, dtype=jnp.int32)
    first_copy = (raw_bits % 32768 < thresholds).astype(jnp.int32)
    second_copy = (raw_bits // 32768 < thresholds).astype(jnp.int32)
    dosage = first_copy + second_copy
    low_row = jax.random.randint(key_low, (1, SNPS), 0, SAMPLES, dtype=jnp.int32)
    high_row = (low_row + 1 + jax.random.randint(key_high, (1, SNPS), 0, SAMPLES - 1, dtype=jnp.int32)) % SAMPLES
    row_index = lax.broadcasted_iota(jnp.int32, (SAMPLES, SNPS), 0)
    dosage = jnp.where(row_index == low_row, 0, dosage)
    dosage = jnp.where(row_index == high_row, 2, dosage)
    return dosage.astype(jnp.int32)


def draw_genotypes(key, part):
    return dosage_matrix(key)


def draw_allele_counts(key, part):
    return jnp.sum(dosage_matrix(key), axis=0).astype(jnp.int32)


def level_of(own_key, shape, cuts, low, top_value):
    level = 1.0
    for dim, blocks in cuts:
        steps = jax.random.uniform(jax.random.fold_in(jax.random.fold_in(own_key, 6), dim), (blocks,), jnp.float32, low / len(cuts), top_value / len(cuts))
        level = level * jnp.repeat(jnp.exp(steps), shape[dim] // blocks).reshape((-1,) + (1,) * (len(shape) - 1 - dim))
    return level


def centred(own_key, shape, scale, limit, pieces=(), held_as=jnp.bfloat16):
    result = jax.random.normal(own_key, shape, jnp.float32) * scale
    if len(pieces) > 0:
        result = level_of(own_key, shape, pieces, -0.22, 0.18) * result
    return jnp.clip(result, min=-limit, max=limit).astype(held_as)


def setup_inputs(seed: int = 0) -> dict:
    keys = jax.random.split(jax.random.key(seed), 7)
    genotypes = draw_genotypes(jax.random.fold_in(keys[6], 71), 0)
    allele_counts = draw_allele_counts(jax.random.fold_in(keys[6], 71), 0)
    ridge_delta = jnp.clip(jnp.exp(jax.random.uniform(keys[2], (RHS,), jnp.float32, math.log(0.3), math.log(3.0))), 0.3, 3.0)
    solution = centred(keys[3], (RHS, SAMPLES), 1.0, 6.0, ((1, 128),), jnp.float32)
    residual = centred(keys[4], (RHS, SAMPLES), 1.0, 6.0, ((1, 128),), jnp.float32)
    direction = centred(keys[5], (RHS, SAMPLES), 1.0, 6.0, ((1, 128),), jnp.float32)
    return {"genotypes": genotypes, "allele_counts": allele_counts, "ridge_delta": ridge_delta, "solution": solution, "residual": residual, "direction": direction}


def standardize(genotypes, allele_counts, samples_all):
    freq = allele_counts.astype(jnp.float32) / (2.0 * samples_all)
    spread = jnp.sqrt(2.0 * freq * (1.0 - freq))
    return (genotypes.astype(jnp.float32) - 2.0 * freq) / spread

def apply_kernel(genotypes, allele_counts, ridge_delta, vectors):

    def one_block(running, block_index):
        start_col = (block_index * SNP_DEV).astype(jnp.int32)
        geno_cols = lax.dynamic_slice_in_dim(genotypes, start_col, SNP_DEV, 1)
        count_cols = lax.dynamic_slice_in_dim(allele_counts, start_col, SNP_DEV, 0)
        scaled = standardize(geno_cols, count_cols, SAMPLES)
        snp_sums = jnp.dot(vectors, scaled, precision=lax.Precision.HIGHEST, preferred_element_type=jnp.float32)
        added = lax.dot_general(snp_sums, scaled, (((1,), (1,)), ((), ())), precision=lax.Precision.HIGHEST, preferred_element_type=jnp.float32)
        return (running + added, None)
    start_sum = jnp.zeros((vectors.shape[0], SAMPLES), jnp.float32)
    totals, _ = lax.scan(one_block, start_sum, jnp.arange(N_SNP, dtype=jnp.int32))
    return totals / SNPS + ridge_delta[:, None] * vectors

def reference(genotypes, allele_counts, ridge_delta, solution, residual, direction):
    norm_now = lax.optimization_barrier(jnp.sum(residual * residual, axis=1))
    for iteration in range(ITERS):
        image_vec = apply_kernel(genotypes, allele_counts, ridge_delta, direction)
        step_size = norm_now / lax.optimization_barrier(jnp.sum(direction * image_vec, axis=1))
        solution = solution + step_size[:, None] * direction
        residual = residual - step_size[:, None] * image_vec
        norm_next = lax.optimization_barrier(jnp.sum(residual * residual, axis=1))
        direction = residual + (norm_next / norm_now)[:, None] * direction
        norm_now = norm_next
    return (solution, residual, direction)
```

```python
import jax
import jax.numpy as jnp
from jax import lax
from jax.sharding import PartitionSpec as P

ITERS = 3
LANES = 128


def from_others(value, axis):
    size = lax.axis_size(axis)
    return [
        lax.ppermute(value, axis, [(i, (i + k) % size) for i in range(size)])
        for k in range(1, size)
    ]


def sum_over(value, axis):
    total = value
    for other in from_others(value, axis):
        total = total + other
    return total


def pieces(value):
    high = lax.reduce_precision(value, 8, 7)
    rest = value - high
    middle = lax.reduce_precision(rest, 8, 7)
    low = rest - middle
    return jnp.concatenate([high, middle, low], axis=0).astype(jnp.bfloat16)


def joined(product):
    k = product.shape[0] // 3
    return product[:k] + (product[k : 2 * k] + product[2 * k :])


def with_scalars(block, *scalars):
    extra = jnp.stack(scalars, axis=1)
    extra = jnp.pad(extra, ((0, 0), (0, LANES - len(scalars))))
    return jnp.concatenate([block, extra], axis=1)


def local(genotypes, allele_counts, ridge, solution, residual, direction):
    rows, snps = genotypes.shape
    own = solution.shape[1]
    samples_all = rows * lax.axis_size("y") * lax.axis_size("c")
    snps_all = snps * lax.axis_size("z") * lax.axis_size("x")
    freq = allele_counts.astype(jnp.float32) / (2.0 * samples_all)
    twice = 2.0 * freq
    inverse = 1.0 / jnp.sqrt(2.0 * freq * (1.0 - freq))
    dosage = genotypes.astype(jnp.bfloat16)

    def forward(v):
        raw = joined(jnp.dot(pieces(v), dosage, preferred_element_type=jnp.float32))
        return (raw - jnp.sum(v, axis=1)[:, None] * twice) * inverse

    def backward(u):
        w = u * inverse
        raw = lax.dot_general(
            pieces(w), dosage, (((1,), (1,)), ((), ())), preferred_element_type=jnp.float32
        )
        return joined(raw) - jnp.sum(w * twice, axis=1)[:, None]

    def over_samp(v):
        return sum_over(sum_over(v, "c"), "y")

    def over_snp(v):
        return sum_over(sum_over(v, "x"), "z")

    z, x = lax.axis_index("z"), lax.axis_index("x")
    both = jnp.concatenate([residual, direction], axis=0)
    part = jnp.zeros((both.shape[0], own * lax.axis_size("x")), jnp.float32)
    part = sum_over(lax.dynamic_update_slice(part, both, (0, x * own)), "x")
    whole = jnp.zeros((both.shape[0], rows), jnp.float32)
    whole = sum_over(lax.dynamic_update_slice(whole, part, (0, z * part.shape[1])), "z")
    k = residual.shape[0]
    r, d = whole[:k], whole[k:]

    def mine(v):
        return lax.dynamic_slice(v, (0, (z * lax.axis_size("x") + x) * own), (k, own))

    norm_now = None
    for iteration in range(ITERS):
        if iteration == 0:
            sums = over_samp(with_scalars(forward(d), jnp.sum(r * r, 1), jnp.sum(d * d, 1)))
            u, norm_now, size = sums[:, :snps], sums[:, snps], sums[:, snps + 1]
        else:
            sums = over_samp(with_scalars(forward(r), jnp.sum(r * r, 1), jnp.sum(r * d, 1)))
            norm_next, cross = sums[:, snps], sums[:, snps + 1]
            ratio = norm_next / norm_now
            u = sums[:, :snps] + ratio[:, None] * u
            d = r + ratio[:, None] * d
            size = norm_next + 2.0 * ratio * cross + ratio * ratio * size
            norm_now = norm_next
        sums = over_snp(with_scalars(backward(u), jnp.sum(u * u, 1)))
        image = sums[:, :rows] / snps_all + ridge[:, None] * d
        step = norm_now / (sums[:, rows] / snps_all + ridge * size)
        solution = solution + step[:, None] * mine(d)
        r = r - step[:, None] * image
    norm_next = over_samp(jnp.sum(r * r, axis=1, keepdims=True))
    r, d = mine(r), mine(d)
    return (solution, r, r + (norm_next / norm_now[:, None]) * d)


def solution(mesh):
    parts = jax.sharding.Mesh(mesh.devices.reshape(4, 2, 4, 4), ("y", "c", "z", "x"))
    vec = P(None, ("y", "c", "z", "x"))
    in_specs = (P(("y", "c"), ("z", "x")), P(("z", "x")), P(), vec, vec, vec)
    return jax.shard_map(
        local, mesh=parts, in_specs=in_specs, out_specs=(vec, vec, vec), check_vma=False
    )
```

```python
import functools

import jax
import jax.numpy as jnp
from jax import lax
from jax.experimental import pallas as pl
from jax.experimental.pallas import tpu as pltpu
from jax.sharding import PartitionSpec as P

ITERS = 3
LANES = 128
TILE = 256
STEP_ROWS = 128
BF16 = jnp.bfloat16
F32 = jnp.float32
VMEM_BYTES = 12 * 2**20


def split(v):
    high = v.astype(BF16).astype(F32)
    rest = v - high
    middle = rest.astype(BF16).astype(F32)
    parts = [high, middle, rest - middle, jnp.zeros_like(v)]
    return jnp.concatenate(parts, axis=0).astype(BF16)


def join(raw):
    return raw[0:4] + (raw[4:8] + raw[8:12])


def lanes_of(*columns):
    lane = lax.broadcasted_iota(jnp.int32, (columns[0].shape[0], LANES), 1)
    block = jnp.zeros(lane.shape, F32)
    for i, column in enumerate(columns):
        block = jnp.where(lane == i, column, block)
    return block


def total(v):
    return jnp.sum(v, axis=1, keepdims=True)


def forward(v, dosage, stats, out):
    parts = split(v)
    shift = total(v)
    snps = dosage.shape[1]
    for n in range(0, snps, TILE):
        at = slice(n, min(n + TILE, snps))
        raw = jnp.dot(parts, dosage[:, at], preferred_element_type=F32)
        out[:, at] = (join(raw) - shift * stats[0:1, at]) * stats[1:2, at]


def backward(u, turned, stats, out):
    w = u * stats[1:2, :]
    parts = split(w)
    shift = total(w * stats[0:1, :])
    rows = turned.shape[1]
    for n in range(0, rows, TILE):
        at = slice(n, n + TILE)
        raw = jnp.dot(parts, turned[:, at], preferred_element_type=F32)
        out[:, at] = join(raw) - shift


def convert_kernel(alleles, genotypes, counts, dosage, stats):
    @pl.loop(0, genotypes.shape[0], step=STEP_ROWS)
    def _(start):
        at = pl.ds(pl.multiple_of(start, STEP_ROWS), STEP_ROWS)
        dosage[at, :] = genotypes[at, :].astype(F32).astype(BF16)

    freq = counts[...].reshape(1, counts.shape[0]).astype(F32) / alleles
    stats[0:1, :] = 2.0 * freq
    stats[1:2, :] = 1.0 / jnp.sqrt(2.0 * freq * (1.0 - freq))
    stats[2:8, :] = jnp.zeros((6, freq.shape[1]), F32)


def turn_kernel(dosage, turned):
    rows, snps = dosage.shape
    for m in range(0, rows, 2 * TILE):
        for n in range(0, snps, LANES):
            turned[n : n + LANES, m : m + 2 * TILE] = dosage[m : m + 2 * TILE, n : n + LANES].T


def first_forward_kernel(own, one, two, three, dosage, stats, r, d, out):
    z, x = lax.axis_index("z"), lax.axis_index("x")
    piece = own.shape[1]
    for k, ref in enumerate((own, one, two, three)):
        at = pl.ds(pl.multiple_of(lax.rem(z + k, 4) * piece, LANES), piece)
        block = pltpu.roll(ref[...], x * (piece // 4), 1)
        r[:, at] = block[0:4]
        d[:, at] = block[4:8]
    snps = dosage.shape[1]
    forward(d[...], dosage, stats, out)
    out[:, snps:] = lanes_of(total(r[...] * r[...]), total(d[...] * d[...]))


def first_backward_kernel(sums, turned, stats, u, scalars, out):
    snps, rows = turned.shape
    u[...] = sums[:, :snps]
    scalars[...] = sums[:, snps:]
    backward(u[...], turned, stats, out)
    out[:, rows:] = lanes_of(total(u[...] * u[...]))


def advance(snps_all, sums, ridge, scalars, r, d, moved):
    rows = r.shape[1]
    norm, size = scalars[:, 0:1], scalars[:, 1:2]
    delta = ridge[:, 0:1]
    curve = sums[:, rows : rows + 1] / snps_all + delta * size
    step = norm / curve
    r_new = r[...] - step * (sums[:, :rows] / snps_all + delta * d[...])
    moved_new = step * d[...]
    if moved is not None:
        moved_new = moved[...] + moved_new
    return r_new, moved_new


def forward_kernel(snps_all, first, *refs):
    sums, ridge, scalars, r, d = refs[:5]
    moved = None if first else refs[5]
    dosage, stats, r_out, moved_out, out = refs[5 if first else 6 :]
    r_new, moved_out[...] = advance(snps_all, sums, ridge, scalars, r, d, moved)
    r_out[...] = r_new
    snps = dosage.shape[1]
    forward(r_new, dosage, stats, out)
    out[:, snps:] = lanes_of(total(r_new * r_new), total(r_new * d[...]))


def backward_kernel(sums, u, r, d, scalars, turned, stats, u_out, d_out, scalars_out, out):
    snps, rows = turned.shape
    norm, size = scalars[:, 0:1], scalars[:, 1:2]
    norm_next, cross = sums[:, snps : snps + 1], sums[:, snps + 1 : snps + 2]
    ratio = norm_next / norm
    u_new = sums[:, :snps] + ratio * u[...]
    u_out[...] = u_new
    d_out[...] = r[...] + ratio * d[...]
    scalars_out[...] = lanes_of(norm_next, norm_next + 2.0 * ratio * cross + ratio * ratio * size)
    backward(u_new, turned, stats, out)
    out[:, rows:] = lanes_of(total(u_new * u_new))


def last_kernel(snps_all, sums, ridge, scalars, r, d, moved, r_out, moved_out, norm):
    r_new, moved_out[...] = advance(snps_all, sums, ridge, scalars, r, d, moved)
    r_out[...] = r_new
    norm[...] = lanes_of(total(r_new * r_new))


def own_kernel(r, d, moved, solution, s_out, r_out, d_out, r_keep):
    rows, own = r.shape[1], solution.shape[1]
    back = rows - (lax.axis_index("z") * lax.axis_size("x") + lax.axis_index("x")) * own
    s_out[...] = solution[...] + pltpu.roll(moved[...], back, 1)[:, :own]
    mine = pltpu.roll(r[...], back, 1)[:, :own]
    r_out[...] = mine
    r_keep[...] = mine
    d_out[...] = pltpu.roll(d[...], back, 1)[:, :own]


def call(kernel, outs, *args, name, dtypes=None, flops=0):
    spec = pl.BlockSpec(memory_space=pltpu.VMEM)
    return pl.pallas_call(
        kernel,
        out_shape=[jax.ShapeDtypeStruct(s, t) for s, t in zip(outs, dtypes or [F32] * len(outs))],
        in_specs=[spec] * len(args),
        out_specs=[spec] * len(outs),
        compiler_params=pltpu.CompilerParams(vmem_limit_bytes=VMEM_BYTES),
        cost_estimate=pl.CostEstimate(flops=flops, bytes_accessed=2**20, transcendentals=0),
        name=name,
    )(*args)


def from_next(value, axis, k):
    size = lax.axis_size(axis)
    return lax.ppermute(value, axis, [((i + k) % size, i) for i in range(size)])


def others(value, axis):
    return [from_next(value, axis, k) for k in range(1, lax.axis_size(axis))]


def sum_over(value, axis):
    size = lax.axis_size(axis)
    swapped = [lax.ppermute(value, axis, [(i, i ^ k) for i in range(size)]) for k in (1, 3, 2)]
    return (value + swapped[0]) + (swapped[1] + swapped[2])


def local(genotypes, allele_counts, ridge, solution, residual, direction):
    rows, snps = genotypes.shape
    k, own = solution.shape
    samples_all = rows * lax.axis_size("y") * lax.axis_size("c")
    snps_all = snps * lax.axis_size("z") * lax.axis_size("x")
    ridge = jnp.broadcast_to(ridge[:, None], (ridge.shape[0], LANES))
    flops = 2 * 16 * rows * snps
    full, short = (k, rows + LANES), (k, snps + LANES)
    vec, row, col, mine = (k, rows), (k, snps), (k, LANES), (k, own)

    genotypes = pltpu.with_memory_space_constraint(genotypes, pltpu.VMEM)
    dosage, stats = call(
        functools.partial(convert_kernel, 2.0 * samples_all),
        ((rows, snps), (8, snps)), genotypes, allele_counts,
        name="convert", dtypes=(BF16, F32), flops=2**35,
    )
    both = jnp.concatenate([residual, direction], axis=0)
    quarter = jnp.concatenate([both] + others(both, "x"), axis=1)
    quarter, stats = lax.optimization_barrier((quarter, stats))
    (turned,) = call(turn_kernel, ((snps, rows),), dosage, name="turn", dtypes=(BF16,), flops=2**32)
    pieces = [quarter] + others(quarter, "z")
    pieces[1], turned = lax.optimization_barrier((pieces[1], turned))
    r, d, sums = call(
        first_forward_kernel, (vec, vec, short), *pieces, dosage, stats,
        name="first_forward", flops=flops,
    )

    def over_samp(v):
        return sum_over(v + from_next(v, "c", 1), "y")

    def over_snp(v):
        return sum_over(sum_over(v, "x"), "z")

    moved = None
    for iteration in range(ITERS):
        sums = over_samp(sums)
        if iteration == 0:
            u, scalars, sums = call(
                first_backward_kernel, (row, col, full), sums, turned, stats,
                name="first_backward", flops=flops,
            )
        else:
            u, d, scalars, sums = call(
                backward_kernel, (row, vec, col, full), sums, u, r, d, scalars, turned, stats,
                name="backward", flops=flops,
            )
        sums = over_snp(sums)
        if iteration < ITERS - 1:
            state = (sums, ridge, scalars, r, d) + (() if moved is None else (moved,))
            r, moved, sums = call(
                functools.partial(forward_kernel, float(snps_all), moved is None),
                (vec, vec, short), *state, dosage, stats, name="forward", flops=flops,
            )
    r, moved, norm = call(
        functools.partial(last_kernel, float(snps_all)), (vec, vec, col),
        sums, ridge, scalars, r, d, moved, name="last",
    )
    solution, r_own, d, r = call(
        own_kernel, (mine, mine, mine, mine), r, d, moved, solution, name="own", flops=2**20
    )
    norm = over_samp(norm)
    return (solution, r_own, r + (norm[:, 0:1] / scalars[:, 0:1]) * d)


def solution(mesh):
    parts = jax.sharding.Mesh(mesh.devices.reshape(4, 2, 4, 4), ("y", "c", "z", "x"))
    vec = P(None, ("y", "c", "z", "x"))
    in_specs = (P(("y", "c"), ("z", "x")), P(("z", "x")), P(), vec, vec, vec)
    return jax.shard_map(
        local, mesh=parts, in_specs=in_specs, out_specs=(vec, vec, vec), check_vma=False
    )
```

```python
import functools

import jax
import jax.numpy as jnp
from jax import lax
from jax.experimental import pallas as pl
from jax.experimental.pallas import tpu as pltpu
from jax.sharding import PartitionSpec as P

ITERS = 3
LANES = 128
TILE = 256
STEP_ROWS = 256
BF16 = jnp.bfloat16
F32 = jnp.float32
VMEM_BYTES = 12 * 2**20


def split(v):
    high = v.astype(BF16).astype(F32)
    rest = v - high
    middle = rest.astype(BF16).astype(F32)
    parts = [high, middle, rest - middle, jnp.zeros_like(v)]
    return jnp.concatenate(parts, axis=0).astype(BF16)


def join(raw):
    return raw[0:4] + (raw[4:8] + raw[8:12])


def lanes_of(*columns):
    lane = lax.broadcasted_iota(jnp.int32, (columns[0].shape[0], LANES), 1)
    block = jnp.zeros(lane.shape, F32)
    for i, column in enumerate(columns):
        block = jnp.where(lane == i, column, block)
    return block


def total(v):
    return jnp.sum(v, axis=1, keepdims=True)


def forward(v, upper, lower, stats, out):
    parts = split(v)
    shift = total(v)
    half, snps = upper.shape
    for n in range(0, snps, TILE):
        at = slice(n, min(n + TILE, snps))
        raw = jnp.dot(parts[:, :half], upper[:, at], preferred_element_type=F32)
        raw += jnp.dot(parts[:, half:], lower[:, at], preferred_element_type=F32)
        out[:, at] = (join(raw) - shift * stats[0:1, at]) * stats[1:2, at]


def backward(u, upper, lower, stats, out):
    w = u * stats[1:2, :]
    parts = split(w)
    shift = total(w * stats[0:1, :])
    half = upper.shape[1]
    for start, turned in ((0, upper), (half, lower)):
        for n in range(0, half, TILE):
            raw = jnp.dot(parts, turned[:, n : n + TILE], preferred_element_type=F32)
            out[:, start + n : start + n + TILE] = join(raw) - shift


def convert_kernel(part, genotypes, dosage, landed, arrived):
    blocks = landed.shape[0]

    def copy(block):
        rows = pl.ds((part * blocks + block) * STEP_ROWS, STEP_ROWS)
        return pltpu.make_async_copy(genotypes.at[rows, :], landed.at[block], arrived.at[block])

    for block in range(blocks):
        copy(block).start()
    for block in range(blocks):
        copy(block).wait()
        rows = slice(block * STEP_ROWS, (block + 1) * STEP_ROWS)
        dosage[rows, :] = landed[block].astype(F32).astype(BF16)


def stats_kernel(alleles, counts, stats):
    freq = counts[...].reshape(1, counts.shape[0]).astype(F32) / alleles
    stats[0:1, :] = 2.0 * freq
    stats[1:2, :] = 1.0 / jnp.sqrt(2.0 * freq * (1.0 - freq))
    stats[2:8, :] = jnp.zeros((6, freq.shape[1]), F32)


def turn_kernel(dosage, turned):
    rows, snps = dosage.shape
    for m in range(0, rows, 2 * TILE):
        for n in range(0, snps, LANES):
            turned[n : n + LANES, m : m + 2 * TILE] = dosage[m : m + 2 * TILE, n : n + LANES].T


def first_forward_kernel(own, one, two, three, upper, lower, stats, r, d, out):
    z, x = lax.axis_index("z"), lax.axis_index("x")
    piece = own.shape[1]
    for k, ref in enumerate((own, one, two, three)):
        at = pl.ds(pl.multiple_of(lax.rem(z + k, 4) * piece, LANES), piece)
        block = pltpu.roll(ref[...], x * (piece // 4), 1)
        r[:, at] = block[0:4]
        d[:, at] = block[4:8]
    snps = upper.shape[1]
    forward(d[...], upper, lower, stats, out)
    out[:, snps:] = lanes_of(total(r[...] * r[...]), total(d[...] * d[...]))


def first_backward_kernel(sums, upper, lower, stats, u, scalars, out):
    snps, half = upper.shape
    u[...] = sums[:, :snps]
    scalars[...] = sums[:, snps:]
    backward(u[...], upper, lower, stats, out)
    out[:, 2 * half :] = lanes_of(total(u[...] * u[...]))


def advance(snps_all, sums, ridge, scalars, r, d, moved):
    rows = r.shape[1]
    norm, size = scalars[:, 0:1], scalars[:, 1:2]
    delta = ridge[:, 0:1]
    curve = sums[:, rows : rows + 1] / snps_all + delta * size
    step = norm / curve
    r_new = r[...] - step * (sums[:, :rows] / snps_all + delta * d[...])
    moved_new = step * d[...]
    if moved is not None:
        moved_new = moved[...] + moved_new
    return r_new, moved_new


def forward_kernel(snps_all, first, *refs):
    sums, ridge, scalars, r, d = refs[:5]
    moved = None if first else refs[5]
    upper, lower, stats, r_out, moved_out, out = refs[5 if first else 6 :]
    r_new, moved_out[...] = advance(snps_all, sums, ridge, scalars, r, d, moved)
    r_out[...] = r_new
    snps = upper.shape[1]
    forward(r_new, upper, lower, stats, out)
    out[:, snps:] = lanes_of(total(r_new * r_new), total(r_new * d[...]))


def backward_kernel(sums, u, r, d, scalars, upper, lower, stats, u_out, d_out, scalars_out, out):
    snps, half = upper.shape
    norm, size = scalars[:, 0:1], scalars[:, 1:2]
    norm_next, cross = sums[:, snps : snps + 1], sums[:, snps + 1 : snps + 2]
    ratio = norm_next / norm
    u_new = sums[:, :snps] + ratio * u[...]
    u_out[...] = u_new
    d_out[...] = r[...] + ratio * d[...]
    scalars_out[...] = lanes_of(norm_next, norm_next + 2.0 * ratio * cross + ratio * ratio * size)
    backward(u_new, upper, lower, stats, out)
    out[:, 2 * half :] = lanes_of(total(u_new * u_new))


def last_kernel(snps_all, sums, ridge, scalars, r, d, moved, r_out, moved_out, norm):
    r_new, moved_out[...] = advance(snps_all, sums, ridge, scalars, r, d, moved)
    r_out[...] = r_new
    norm[...] = lanes_of(total(r_new * r_new))


def own_kernel(r, d, moved, solution, s_out, r_out, d_out, r_keep):
    rows, own = r.shape[1], solution.shape[1]
    back = rows - (lax.axis_index("z") * lax.axis_size("x") + lax.axis_index("x")) * own
    s_out[...] = solution[...] + pltpu.roll(moved[...], back, 1)[:, :own]
    mine = pltpu.roll(r[...], back, 1)[:, :own]
    r_out[...] = mine
    r_keep[...] = mine
    d_out[...] = pltpu.roll(d[...], back, 1)[:, :own]


def call(kernel, outs, *args, name, dtypes=None, flops=0):
    spec = pl.BlockSpec(memory_space=pltpu.VMEM)
    return pl.pallas_call(
        kernel,
        out_shape=[jax.ShapeDtypeStruct(s, t) for s, t in zip(outs, dtypes or [F32] * len(outs))],
        in_specs=[spec] * len(args),
        out_specs=[spec] * len(outs),
        compiler_params=pltpu.CompilerParams(vmem_limit_bytes=VMEM_BYTES),
        cost_estimate=pl.CostEstimate(flops=flops, bytes_accessed=2**20, transcendentals=0),
        name=name,
    )(*args)


def from_next(value, axis, k):
    size = lax.axis_size(axis)
    return lax.ppermute(value, axis, [((i + k) % size, i) for i in range(size)])


def others(value, axis):
    return [from_next(value, axis, k) for k in range(1, lax.axis_size(axis))]


def sum_over(value, axis):
    size = lax.axis_size(axis)
    swapped = [lax.ppermute(value, axis, [(i, i ^ k) for i in range(size)]) for k in (1, 3, 2)]
    return (value + swapped[0]) + (swapped[1] + swapped[2])


def local(genotypes, allele_counts, ridge, solution, residual, direction):
    rows, snps = genotypes.shape
    k, own = solution.shape
    samples_all = rows * lax.axis_size("y") * lax.axis_size("c")
    snps_all = snps * lax.axis_size("z") * lax.axis_size("x")
    ridge = jnp.broadcast_to(ridge[:, None], (ridge.shape[0], LANES))
    flops = 2 * 16 * rows * snps
    full, short = (k, rows + LANES), (k, snps + LANES)
    vec, row, col, mine = (k, rows), (k, snps), (k, LANES), (k, own)

    half = rows // 2
    steps = half // STEP_ROWS
    genotypes = pltpu.with_memory_space_constraint(genotypes, pltpu.HBM)

    def converted(part):
        return pl.pallas_call(
            functools.partial(convert_kernel, part),
            out_shape=jax.ShapeDtypeStruct((half, snps), BF16),
            in_specs=[pl.BlockSpec(memory_space=pltpu.HBM)],
            out_specs=pl.BlockSpec(memory_space=pltpu.VMEM),
            scratch_shapes=[
                pltpu.VMEM((steps, STEP_ROWS, snps), jnp.int32),
                pltpu.SemaphoreType.DMA((steps,)),
            ],
            compiler_params=pltpu.CompilerParams(vmem_limit_bytes=2 * VMEM_BYTES),
            cost_estimate=pl.CostEstimate(
                flops=half * snps, bytes_accessed=half * snps * 6, transcendentals=0
            ),
            name="convert",
        )(genotypes)

    (stats,) = call(
        functools.partial(stats_kernel, 2.0 * samples_all), ((8, snps),), allele_counts, name="stats"
    )
    both = jnp.concatenate([residual, direction], axis=0)
    upper = converted(0)
    quarter = jnp.concatenate([both] + others(both, "x"), axis=1)
    quarter, upper = lax.optimization_barrier((quarter, upper))
    lower = converted(1)
    pieces = [quarter] + others(quarter, "z")
    pieces[1], lower = lax.optimization_barrier((pieces[1], lower))
    r, d, sums = call(
        first_forward_kernel, (vec, vec, short), *pieces, upper, lower, stats,
        name="first_forward", flops=flops,
    )
    turned = [
        call(turn_kernel, ((snps, half),), part, name="turn", dtypes=(BF16,), flops=2**30)[0]
        for part in (upper, lower)
    ]

    def over_samp(v):
        return sum_over(v + from_next(v, "c", 1), "y")

    def over_snp(v):
        return sum_over(sum_over(v, "x"), "z")

    moved = None
    for iteration in range(ITERS):
        sums = over_samp(sums)
        if iteration == 0:
            u, scalars, sums = call(
                first_backward_kernel, (row, col, full), sums, *turned, stats,
                name="first_backward", flops=flops,
            )
        else:
            u, d, scalars, sums = call(
                backward_kernel, (row, vec, col, full), sums, u, r, d, scalars, *turned, stats,
                name="backward", flops=flops,
            )
        sums = over_snp(sums)
        if iteration < ITERS - 1:
            state = (sums, ridge, scalars, r, d) + (() if moved is None else (moved,))
            r, moved, sums = call(
                functools.partial(forward_kernel, float(snps_all), moved is None),
                (vec, vec, short), *state, upper, lower, stats, name="forward", flops=flops,
            )
    r, moved, norm = call(
        functools.partial(last_kernel, float(snps_all)), (vec, vec, col),
        sums, ridge, scalars, r, d, moved, name="last",
    )
    solution, r_own, d, r = call(
        own_kernel, (mine, mine, mine, mine), r, d, moved, solution, name="own", flops=2**20
    )
    norm = over_samp(norm)
    return (solution, r_own, r + (norm[:, 0:1] / scalars[:, 0:1]) * d)


def solution(mesh):
    parts = jax.sharding.Mesh(mesh.devices.reshape(4, 2, 4, 4), ("y", "c", "z", "x"))
    vec = P(None, ("y", "c", "z", "x"))
    in_specs = (P(("y", "c"), ("z", "x")), P(("z", "x")), P(), vec, vec, vec)
    return jax.shard_map(
        local, mesh=parts, in_specs=in_specs, out_specs=(vec, vec, vec), check_vma=False
    )
```

```python
import functools

import jax
import jax.numpy as jnp
from jax import lax
from jax.experimental import pallas as pl
from jax.experimental.pallas import tpu as pltpu
from jax.sharding import PartitionSpec as P

ITERS = 3
LANES = 128
TILE = 256
STEP_ROWS = 256
BF16 = jnp.bfloat16
F32 = jnp.float32
VMEM_BYTES = 12 * 2**20


def split(v):
    high = v.astype(BF16).astype(F32)
    rest = v - high
    middle = rest.astype(BF16).astype(F32)
    parts = [high, middle, rest - middle, jnp.zeros_like(v)]
    return jnp.concatenate(parts, axis=0).astype(BF16)


def join(raw):
    return raw[0:4] + (raw[4:8] + raw[8:12])


def lanes_of(*columns):
    lane = lax.broadcasted_iota(jnp.int32, (columns[0].shape[0], LANES), 1)
    block = jnp.zeros(lane.shape, F32)
    for i, column in enumerate(columns):
        block = jnp.where(lane == i, column, block)
    return block


def total(v):
    return jnp.sum(v, axis=1, keepdims=True)


def forward(v, upper, lower, stats, out):
    parts = split(v)
    shift = total(v)
    half, snps = upper.shape
    for n in range(0, snps, TILE):
        at = slice(n, min(n + TILE, snps))
        raw = jnp.dot(parts[:, :half], upper[:, at], preferred_element_type=F32)
        raw += jnp.dot(parts[:, half:], lower[:, at], preferred_element_type=F32)
        out[:, at] = (join(raw) - shift * stats[0:1, at]) * stats[1:2, at]


def backward(u, upper, lower, stats, out):
    w = u * stats[1:2, :]
    parts = split(w)
    shift = total(w * stats[0:1, :])
    half = upper.shape[1]
    for start, turned in ((0, upper), (half, lower)):
        for n in range(0, half, TILE):
            raw = jnp.dot(parts, turned[:, n : n + TILE], preferred_element_type=F32)
            out[:, start + n : start + n + TILE] = join(raw) - shift


def convert_kernel(part, genotypes, dosage, landed, arrived):
    blocks = landed.shape[0]

    def copy(block):
        rows = pl.ds((part * blocks + block) * STEP_ROWS, STEP_ROWS)
        return pltpu.make_async_copy(genotypes.at[rows, :], landed.at[block], arrived.at[block])

    for block in range(blocks):
        copy(block).start()
    for block in range(blocks):
        copy(block).wait()
        rows = slice(block * STEP_ROWS, (block + 1) * STEP_ROWS)
        dosage[rows, :] = landed[block].astype(F32).astype(BF16)


def stats_kernel(alleles, counts, stats):
    freq = counts[...].reshape(1, counts.shape[0]).astype(F32) / alleles
    stats[0:1, :] = 2.0 * freq
    stats[1:2, :] = 1.0 / jnp.sqrt(2.0 * freq * (1.0 - freq))
    stats[2:8, :] = jnp.zeros((6, freq.shape[1]), F32)


def turn_kernel(dosage, turned):
    rows, snps = dosage.shape
    for m in range(0, rows, 2 * TILE):
        for n in range(0, snps, LANES):
            turned[n : n + LANES, m : m + 2 * TILE] = dosage[m : m + 2 * TILE, n : n + LANES].T


def first_forward_kernel(zero, one, two, three, upper, lower, stats, r, d, out):
    z, x = lax.axis_index("z"), lax.axis_index("x")
    piece = zero.shape[1]
    half, own = piece // 2, piece // 4
    for k, ref in enumerate((zero, one, two, three)):
        at = pl.ds(pl.multiple_of((z ^ k) * piece, LANES), piece)
        pairs = [pltpu.roll(ref[:, i : i + half], (x & 1) * own, 1) for i in (0, half)]
        block = pltpu.roll(jnp.concatenate(pairs, axis=1), (x >> 1) * half, 1)
        r[:, at] = block[0:4]
        d[:, at] = block[4:8]
    snps = upper.shape[1]
    forward(d[...], upper, lower, stats, out)
    out[:, snps:] = lanes_of(total(r[...] * r[...]), total(d[...] * d[...]))


def first_backward_kernel(sums, upper, lower, stats, u, scalars, out):
    snps, half = upper.shape
    u[...] = sums[:, :snps]
    scalars[...] = sums[:, snps:]
    backward(u[...], upper, lower, stats, out)
    out[:, 2 * half :] = lanes_of(total(u[...] * u[...]))


def advance(snps_all, sums, ridge, scalars, r, d, moved):
    rows = r.shape[1]
    norm, size = scalars[:, 0:1], scalars[:, 1:2]
    delta = ridge[:, 0:1]
    curve = sums[:, rows : rows + 1] / snps_all + delta * size
    step = norm / curve
    r_new = r[...] - step * (sums[:, :rows] / snps_all + delta * d[...])
    moved_new = step * d[...]
    if moved is not None:
        moved_new = moved[...] + moved_new
    return r_new, moved_new


def forward_kernel(snps_all, first, *refs):
    sums, ridge, scalars, r, d = refs[:5]
    moved = None if first else refs[5]
    upper, lower, stats, r_out, moved_out, out = refs[5 if first else 6 :]
    r_new, moved_out[...] = advance(snps_all, sums, ridge, scalars, r, d, moved)
    r_out[...] = r_new
    snps = upper.shape[1]
    forward(r_new, upper, lower, stats, out)
    out[:, snps:] = lanes_of(total(r_new * r_new), total(r_new * d[...]))


def backward_kernel(sums, u, r, d, scalars, upper, lower, stats, u_out, d_out, scalars_out, out):
    snps, half = upper.shape
    norm, size = scalars[:, 0:1], scalars[:, 1:2]
    norm_next, cross = sums[:, snps : snps + 1], sums[:, snps + 1 : snps + 2]
    ratio = norm_next / norm
    u_new = sums[:, :snps] + ratio * u[...]
    u_out[...] = u_new
    d_out[...] = r[...] + ratio * d[...]
    scalars_out[...] = lanes_of(norm_next, norm_next + 2.0 * ratio * cross + ratio * ratio * size)
    backward(u_new, upper, lower, stats, out)
    out[:, 2 * half :] = lanes_of(total(u_new * u_new))


def last_kernel(snps_all, sums, ridge, scalars, r, d, moved, r_out, moved_out, norm):
    r_new, moved_out[...] = advance(snps_all, sums, ridge, scalars, r, d, moved)
    r_out[...] = r_new
    norm[...] = lanes_of(total(r_new * r_new))


def own_kernel(r, d, moved, solution, s_out, r_out, d_out, r_keep):
    rows, own = r.shape[1], solution.shape[1]
    back = rows - (lax.axis_index("z") * lax.axis_size("x") + lax.axis_index("x")) * own
    s_out[...] = solution[...] + pltpu.roll(moved[...], back, 1)[:, :own]
    mine = pltpu.roll(r[...], back, 1)[:, :own]
    r_out[...] = mine
    r_keep[...] = mine
    d_out[...] = pltpu.roll(d[...], back, 1)[:, :own]


def call(kernel, outs, *args, name, dtypes=None, flops=0):
    spec = pl.BlockSpec(memory_space=pltpu.VMEM)
    return pl.pallas_call(
        kernel,
        out_shape=[jax.ShapeDtypeStruct(s, t) for s, t in zip(outs, dtypes or [F32] * len(outs))],
        in_specs=[spec] * len(args),
        out_specs=[spec] * len(outs),
        compiler_params=pltpu.CompilerParams(vmem_limit_bytes=VMEM_BYTES),
        cost_estimate=pl.CostEstimate(flops=flops, bytes_accessed=2**20, transcendentals=0),
        name=name,
    )(*args)


def swap_cores(value):
    return lax.ppermute(value, "c", [(0, 1), (1, 0)])


def swap_across(value, axis, k):
    names = ("y", "c") if axis == "y" else ("c", axis)
    size, chips = 2 * lax.axis_size(axis), lax.axis_size(axis)
    if axis == "y":
        pairs = [(i, i ^ (2 * k + 1)) for i in range(size)]
    else:
        pairs = [(i, i ^ (chips + k)) for i in range(size)]
    return lax.ppermute(value, names, pairs)


def crossed(value, axis):
    one, three, two = [swap_across(value, axis, k) for k in (1, 3, 2)]
    return [swap_cores(value), one, two, three]


def sum_crossed(value, axis):
    zero, one, two, three = crossed(value, axis)
    return (zero + one) + (three + two)


def local(genotypes, allele_counts, ridge, solution, residual, direction):
    rows, snps = genotypes.shape
    k, own = solution.shape
    samples_all = rows * lax.axis_size("y") * lax.axis_size("c")
    snps_all = snps * lax.axis_size("z") * lax.axis_size("x")
    ridge = jnp.broadcast_to(ridge[:, None], (ridge.shape[0], LANES))
    flops = 2 * 16 * rows * snps
    full, short = (k, rows + LANES), (k, snps + LANES)
    vec, row, col, mine = (k, rows), (k, snps), (k, LANES), (k, own)

    half = rows // 2
    steps = half // STEP_ROWS
    genotypes = pltpu.with_memory_space_constraint(genotypes, pltpu.HBM)

    def converted(part):
        return pl.pallas_call(
            functools.partial(convert_kernel, part),
            out_shape=jax.ShapeDtypeStruct((half, snps), BF16),
            in_specs=[pl.BlockSpec(memory_space=pltpu.HBM)],
            out_specs=pl.BlockSpec(memory_space=pltpu.VMEM),
            scratch_shapes=[
                pltpu.VMEM((steps, STEP_ROWS, snps), jnp.int32),
                pltpu.SemaphoreType.DMA((steps,)),
            ],
            compiler_params=pltpu.CompilerParams(vmem_limit_bytes=2 * VMEM_BYTES),
            cost_estimate=pl.CostEstimate(
                flops=half * snps, bytes_accessed=half * snps * 6, transcendentals=0
            ),
            name="convert",
        )(genotypes)

    (stats,) = call(
        functools.partial(stats_kernel, 2.0 * samples_all), ((8, snps),), allele_counts, name="stats"
    )
    both = jnp.concatenate([residual, direction], axis=0)
    upper = converted(0)
    quarter = jnp.concatenate(crossed(both, "x"), axis=1)
    quarter, upper = lax.optimization_barrier((quarter, upper))
    lower = converted(1)
    pieces = crossed(quarter, "z")
    pieces[1], lower = lax.optimization_barrier((pieces[1], lower))
    r, d, sums = call(
        first_forward_kernel, (vec, vec, short), *pieces, upper, lower, stats,
        name="first_forward", flops=flops,
    )
    turned = [
        call(turn_kernel, ((snps, half),), part, name="turn", dtypes=(BF16,), flops=2**30)[0]
        for part in (upper, lower)
    ]

    def over_samp(v):
        v = v + swap_cores(v)
        one, three, two = [swap_across(v, "y", k) for k in (1, 3, 2)]
        return (v + one) + (three + two)

    def over_snp(v):
        return sum_crossed(sum_crossed(v, "x"), "z")

    moved = None
    for iteration in range(ITERS):
        sums = over_samp(sums)
        if iteration == 0:
            u, scalars, sums = call(
                first_backward_kernel, (row, col, full), sums, *turned, stats,
                name="first_backward", flops=flops,
            )
        else:
            u, d, scalars, sums = call(
                backward_kernel, (row, vec, col, full), sums, u, r, d, scalars, *turned, stats,
                name="backward", flops=flops,
            )
        sums = over_snp(sums)
        if iteration < ITERS - 1:
            state = (sums, ridge, scalars, r, d) + (() if moved is None else (moved,))
            r, moved, sums = call(
                functools.partial(forward_kernel, float(snps_all), moved is None),
                (vec, vec, short), *state, upper, lower, stats, name="forward", flops=flops,
            )
    r, moved, norm = call(
        functools.partial(last_kernel, float(snps_all)), (vec, vec, col),
        sums, ridge, scalars, r, d, moved, name="last",
    )
    solution, r_own, d, r = call(
        own_kernel, (mine, mine, mine, mine), r, d, moved, solution, name="own", flops=2**20
    )
    norm = over_samp(norm)
    return (solution, r_own, r + (norm[:, 0:1] / scalars[:, 0:1]) * d)


def solution(mesh):
    parts = jax.sharding.Mesh(mesh.devices.reshape(4, 2, 4, 4), ("y", "c", "z", "x"))
    vec = P(None, ("y", "c", "z", "x"))
    in_specs = (P(("y", "c"), ("z", "x")), P(("z", "x")), P(), vec, vec, vec)
    return jax.shard_map(
        local, mesh=parts, in_specs=in_specs, out_specs=(vec, vec, vec), check_vma=False
    )
```

```python
import functools

import jax
import jax.numpy as jnp
from jax import lax
from jax.experimental import pallas as pl
from jax.experimental.pallas import tpu as pltpu
from jax.sharding import PartitionSpec as P

ITERS = 3
LANES = 128
TILE = 256
STEP_ROWS = 256
BF16 = jnp.bfloat16
F32 = jnp.float32
VMEM_BYTES = 12 * 2**20


def split(v):
    high = v.astype(BF16).astype(F32)
    rest = v - high
    middle = rest.astype(BF16).astype(F32)
    parts = [high, middle, rest - middle, jnp.zeros_like(v)]
    return jnp.concatenate(parts, axis=0).astype(BF16)


def join(raw):
    return raw[0:4] + (raw[4:8] + raw[8:12])


def lanes_of(*columns):
    lane = lax.broadcasted_iota(jnp.int32, (columns[0].shape[0], LANES), 1)
    block = jnp.zeros(lane.shape, F32)
    for i, column in enumerate(columns):
        block = jnp.where(lane == i, column, block)
    return block


def total(v):
    return jnp.sum(v, axis=1, keepdims=True)


def forward(v, upper, lower, stats, out):
    parts = split(v)
    shift = total(v)
    half, snps = upper.shape
    for n in range(0, snps, TILE):
        at = slice(n, min(n + TILE, snps))
        raw = jnp.dot(parts[:, :half], upper[:, at], preferred_element_type=F32)
        raw += jnp.dot(parts[:, half:], lower[:, at], preferred_element_type=F32)
        out[:, at] = (join(raw) - shift * stats[0:1, at]) * stats[1:2, at]


def backward(u, upper, lower, stats, out):
    w = u * stats[1:2, :]
    parts = split(w)
    shift = total(w * stats[0:1, :])
    half = upper.shape[1]
    for start, turned in ((0, upper), (half, lower)):
        for n in range(0, half, TILE):
            raw = jnp.dot(parts, turned[:, n : n + TILE], preferred_element_type=F32)
            out[:, start + n : start + n + TILE] = join(raw) - shift


def convert_kernel(part, genotypes, dosage, landed, arrived):
    blocks = landed.shape[0]

    def copy(block):
        rows = pl.ds((part * blocks + block) * STEP_ROWS, STEP_ROWS)
        return pltpu.make_async_copy(genotypes.at[rows, :], landed.at[block], arrived.at[block])

    for block in range(blocks):
        copy(block).start()
    for block in range(blocks):
        copy(block).wait()
        rows = slice(block * STEP_ROWS, (block + 1) * STEP_ROWS)
        dosage[rows, :] = landed[block].astype(F32).astype(BF16)


def stats_kernel(alleles, counts, stats):
    freq = counts[...].reshape(1, counts.shape[0]).astype(F32) / alleles
    stats[0:1, :] = 2.0 * freq
    stats[1:2, :] = 1.0 / jnp.sqrt(2.0 * freq * (1.0 - freq))
    stats[2:8, :] = jnp.zeros((6, freq.shape[1]), F32)


def turn_kernel(dosage, turned):
    rows, snps = dosage.shape
    for m in range(0, rows, 2 * TILE):
        for n in range(0, snps, LANES):
            turned[n : n + LANES, m : m + 2 * TILE] = dosage[m : m + 2 * TILE, n : n + LANES].T


def first_forward_kernel(zero, one, two, three, upper, lower, stats, r, d, out):
    z, x = lax.axis_index("z"), lax.axis_index("x")
    piece = zero.shape[1]
    half, own = piece // 2, piece // 4
    for k, ref in enumerate((zero, one, two, three)):
        at = pl.ds(pl.multiple_of((z ^ k) * piece, LANES), piece)
        pairs = [pltpu.roll(ref[:, i : i + half], (x & 1) * own, 1) for i in (0, half)]
        block = pltpu.roll(jnp.concatenate(pairs, axis=1), (x >> 1) * half, 1)
        r[:, at] = block[0:4]
        d[:, at] = block[4:8]
    snps = upper.shape[1]
    forward(d[...], upper, lower, stats, out)
    out[:, snps:] = lanes_of(total(r[...] * r[...]), total(d[...] * d[...]))


def first_backward_kernel(sums, upper, lower, stats, u, scalars, out):
    snps, half = upper.shape
    u[...] = sums[:, :snps]
    scalars[...] = sums[:, snps:]
    backward(u[...], upper, lower, stats, out)
    out[:, 2 * half :] = lanes_of(total(u[...] * u[...]))


def advance(snps_all, sums, ridge, scalars, r, d, moved):
    rows = r.shape[1]
    norm, size = scalars[:, 0:1], scalars[:, 1:2]
    delta = ridge[:, 0:1]
    curve = sums[:, rows : rows + 1] / snps_all + delta * size
    step = norm / curve
    r_new = r[...] - step * (sums[:, :rows] / snps_all + delta * d[...])
    moved_new = step * d[...]
    if moved is not None:
        moved_new = moved[...] + moved_new
    return r_new, moved_new


def forward_kernel(snps_all, first, *refs):
    sums, ridge, scalars, r, d = refs[:5]
    moved = None if first else refs[5]
    upper, lower, stats, r_out, moved_out, out = refs[5 if first else 6 :]
    r_new, moved_out[...] = advance(snps_all, sums, ridge, scalars, r, d, moved)
    r_out[...] = r_new
    snps = upper.shape[1]
    forward(r_new, upper, lower, stats, out)
    out[:, snps:] = lanes_of(total(r_new * r_new), total(r_new * d[...]))


def backward_kernel(sums, u, r, d, scalars, upper, lower, stats, u_out, d_out, scalars_out, out):
    snps, half = upper.shape
    norm, size = scalars[:, 0:1], scalars[:, 1:2]
    norm_next, cross = sums[:, snps : snps + 1], sums[:, snps + 1 : snps + 2]
    ratio = norm_next / norm
    u_new = sums[:, :snps] + ratio * u[...]
    u_out[...] = u_new
    d_out[...] = r[...] + ratio * d[...]
    scalars_out[...] = lanes_of(norm_next, norm_next + 2.0 * ratio * cross + ratio * ratio * size)
    backward(u_new, upper, lower, stats, out)
    out[:, 2 * half :] = lanes_of(total(u_new * u_new))


def last_kernel(snps_all, sums, ridge, scalars, r, d, moved, r_out, moved_out, norm):
    r_new, moved_out[...] = advance(snps_all, sums, ridge, scalars, r, d, moved)
    r_out[...] = r_new
    norm[...] = lanes_of(total(r_new * r_new))


def own_kernel(r, d, moved, solution, s_out, r_out, d_out, r_keep):
    rows, own = r.shape[1], solution.shape[1]
    back = rows - (lax.axis_index("z") * lax.axis_size("x") + lax.axis_index("x")) * own
    s_out[...] = solution[...] + pltpu.roll(moved[...], back, 1)[:, :own]
    mine = pltpu.roll(r[...], back, 1)[:, :own]
    r_out[...] = mine
    r_keep[...] = mine
    d_out[...] = pltpu.roll(d[...], back, 1)[:, :own]


def call(kernel, outs, *args, name, dtypes=None, flops=0):
    spec = pl.BlockSpec(memory_space=pltpu.VMEM)
    return pl.pallas_call(
        kernel,
        out_shape=[jax.ShapeDtypeStruct(s, t) for s, t in zip(outs, dtypes or [F32] * len(outs))],
        in_specs=[spec] * len(args),
        out_specs=[spec] * len(outs),
        compiler_params=pltpu.CompilerParams(vmem_limit_bytes=VMEM_BYTES),
        cost_estimate=pl.CostEstimate(flops=flops, bytes_accessed=2**20, transcendentals=0),
        name=name,
    )(*args)


def swap_cores(value):
    return lax.ppermute(value, "c", [(0, 1), (1, 0)])


def swap_across(value, axis, k):
    names = ("y", "c") if axis == "y" else ("c", axis)
    size, chips = 2 * lax.axis_size(axis), lax.axis_size(axis)
    if axis == "y":
        pairs = [(i, i ^ (2 * k + 1)) for i in range(size)]
    else:
        pairs = [(i, i ^ (chips + k)) for i in range(size)]
    return lax.ppermute(value, names, pairs)


def crossed(value, axis):
    one, three, two = [swap_across(value, axis, k) for k in (1, 3, 2)]
    return [swap_cores(value), one, two, three]


def sum_crossed(value, axis):
    zero, one, two, three = crossed(value, axis)
    return (zero + one) + (three + two)


def local(genotypes, allele_counts, ridge, solution, residual, direction):
    rows, snps = genotypes.shape
    k, own = solution.shape
    samples_all = rows * lax.axis_size("y") * lax.axis_size("c")
    snps_all = snps * lax.axis_size("z") * lax.axis_size("x")
    ridge = jnp.broadcast_to(ridge[:, None], (ridge.shape[0], LANES))
    flops = 2 * 16 * rows * snps
    full, short = (k, rows + LANES), (k, snps + LANES)
    vec, row, col, mine = (k, rows), (k, snps), (k, LANES), (k, own)

    half = rows // 2
    steps = half // STEP_ROWS
    genotypes = pltpu.with_memory_space_constraint(genotypes, pltpu.HBM)

    def converted(part):
        return pl.pallas_call(
            functools.partial(convert_kernel, part),
            out_shape=jax.ShapeDtypeStruct((half, snps), BF16),
            in_specs=[pl.BlockSpec(memory_space=pltpu.HBM)],
            out_specs=pl.BlockSpec(memory_space=pltpu.VMEM),
            scratch_shapes=[
                pltpu.VMEM((steps, STEP_ROWS, snps), jnp.int32),
                pltpu.SemaphoreType.DMA((steps,)),
            ],
            compiler_params=pltpu.CompilerParams(vmem_limit_bytes=2 * VMEM_BYTES),
            cost_estimate=pl.CostEstimate(
                flops=half * snps, bytes_accessed=half * snps * 6, transcendentals=0
            ),
            name="convert",
        )(genotypes)

    (stats,) = call(
        functools.partial(stats_kernel, 2.0 * samples_all), ((8, snps),), allele_counts, name="stats"
    )
    both = jnp.concatenate([residual, direction], axis=0)
    upper = converted(0)
    quarter = jnp.concatenate(crossed(both, "x"), axis=1)
    quarter, upper = lax.optimization_barrier((quarter, upper))
    lower = converted(1)
    pieces = crossed(quarter, "z")
    *pieces, lower = lax.optimization_barrier((*pieces, lower))
    r, d, sums = call(
        first_forward_kernel, (vec, vec, short), *pieces, upper, lower, stats,
        name="first_forward", flops=flops,
    )
    turned = [
        call(turn_kernel, ((snps, half),), part, name="turn", dtypes=(BF16,), flops=2**30)[0]
        for part in (upper, lower)
    ]

    def over_samp(v):
        v = v + swap_cores(v)
        one, three, two = [swap_across(v, "y", k) for k in (1, 3, 2)]
        return (v + one) + (three + two)

    def over_snp(v):
        return sum_crossed(sum_crossed(v, "x"), "z")

    moved = None
    for iteration in range(ITERS):
        sums = over_samp(sums)
        if iteration == 0:
            u, scalars, sums = call(
                first_backward_kernel, (row, col, full), sums, *turned, stats,
                name="first_backward", flops=flops,
            )
        else:
            u, d, scalars, sums = call(
                backward_kernel, (row, vec, col, full), sums, u, r, d, scalars, *turned, stats,
                name="backward", flops=flops,
            )
        sums = over_snp(sums)
        if iteration < ITERS - 1:
            state = (sums, ridge, scalars, r, d) + (() if moved is None else (moved,))
            r, moved, sums = call(
                functools.partial(forward_kernel, float(snps_all), moved is None),
                (vec, vec, short), *state, upper, lower, stats, name="forward", flops=flops,
            )
    r, moved, norm = call(
        functools.partial(last_kernel, float(snps_all)), (vec, vec, col),
        sums, ridge, scalars, r, d, moved, name="last",
    )
    solution, r_own, d, r = call(
        own_kernel, (mine, mine, mine, mine), r, d, moved, solution, name="own", flops=2**20
    )
    norm = over_samp(norm)
    return (solution, r_own, r + (norm[:, 0:1] / scalars[:, 0:1]) * d)


def solution(mesh):
    parts = jax.sharding.Mesh(mesh.devices.reshape(4, 2, 4, 4), ("y", "c", "z", "x"))
    vec = P(None, ("y", "c", "z", "x"))
    in_specs = (P(("y", "c"), ("z", "x")), P(("z", "x")), P(), vec, vec, vec)
    return jax.shard_map(
        local, mesh=parts, in_specs=in_specs, out_specs=(vec, vec, vec), check_vma=False
    )
```

```python
import functools

import jax
import jax.numpy as jnp
from jax import lax
from jax.experimental import pallas as pl
from jax.experimental.pallas import tpu as pltpu
from jax.sharding import PartitionSpec as P

ITERS = 3
LANES = 128
TILE = 256
STEP_ROWS = 256
BF16 = jnp.bfloat16
F32 = jnp.float32
VMEM_BYTES = 12 * 2**20


def split(v):
    high = v.astype(BF16).astype(F32)
    rest = v - high
    middle = rest.astype(BF16).astype(F32)
    parts = [high, middle, rest - middle, jnp.zeros_like(v)]
    return jnp.concatenate(parts, axis=0).astype(BF16)


def join(raw):
    return raw[0:4] + (raw[4:8] + raw[8:12])


def lanes_of(*columns):
    lane = lax.broadcasted_iota(jnp.int32, (columns[0].shape[0], LANES), 1)
    block = jnp.zeros(lane.shape, F32)
    for i, column in enumerate(columns):
        block = jnp.where(lane == i, column, block)
    return block


def total(v):
    return jnp.sum(v, axis=1, keepdims=True)


def forward(v, upper, lower, stats, out):
    parts = split(v)
    shift = total(v)
    half, snps = upper.shape
    for n in range(0, snps, TILE):
        at = slice(n, min(n + TILE, snps))
        raw = jnp.dot(parts[:, :half], upper[:, at], preferred_element_type=F32)
        raw += jnp.dot(parts[:, half:], lower[:, at], preferred_element_type=F32)
        out[:, at] = (join(raw) - shift * stats[0:1, at]) * stats[1:2, at]


def backward(u, upper, lower, stats, out):
    w = u * stats[1:2, :]
    parts = split(w)
    shift = total(w * stats[0:1, :])
    half = upper.shape[1]
    for start, turned in ((0, upper), (half, lower)):
        for n in range(0, half, TILE):
            raw = jnp.dot(parts, turned[:, n : n + TILE], preferred_element_type=F32)
            out[:, start + n : start + n + TILE] = join(raw) - shift


def convert_kernel(part, genotypes, dosage, landed, arrived):
    blocks = landed.shape[0]

    def copy(block):
        rows = pl.ds((part * blocks + block) * STEP_ROWS, STEP_ROWS)
        return pltpu.make_async_copy(genotypes.at[rows, :], landed.at[block], arrived.at[block])

    for block in range(blocks):
        copy(block).start()
    for block in range(blocks):
        copy(block).wait()
        rows = slice(block * STEP_ROWS, (block + 1) * STEP_ROWS)
        dosage[rows, :] = landed[block].astype(F32).astype(BF16)


def stats_kernel(alleles, counts, stats):
    freq = counts[...].reshape(1, counts.shape[0]).astype(F32) / alleles
    stats[0:1, :] = 2.0 * freq
    stats[1:2, :] = 1.0 / jnp.sqrt(2.0 * freq * (1.0 - freq))
    stats[2:8, :] = jnp.zeros((6, freq.shape[1]), F32)


def turn_kernel(dosage, turned):
    rows, snps = dosage.shape
    for m in range(0, rows, 2 * TILE):
        for n in range(0, snps, LANES):
            turned[n : n + LANES, m : m + 2 * TILE] = dosage[m : m + 2 * TILE, n : n + LANES].T


def first_forward_kernel(zero, one, two, three, upper, lower, stats, r, d, out):
    z, x = lax.axis_index("z"), lax.axis_index("x")
    piece = zero.shape[1]
    half, own = piece // 2, piece // 4
    for k, ref in enumerate((zero, one, two, three)):
        at = pl.ds(pl.multiple_of((z ^ k) * piece, LANES), piece)
        pairs = [pltpu.roll(ref[:, i : i + half], (x & 1) * own, 1) for i in (0, half)]
        block = pltpu.roll(jnp.concatenate(pairs, axis=1), (x >> 1) * half, 1)
        r[:, at] = block[0:4]
        d[:, at] = block[4:8]
    snps = upper.shape[1]
    forward(d[...], upper, lower, stats, out)
    out[:, snps:] = lanes_of(total(r[...] * r[...]), total(d[...] * d[...]))


def first_backward_kernel(sums, upper, lower, stats, u, scalars, out):
    snps, half = upper.shape
    u[...] = sums[:, :snps]
    scalars[...] = sums[:, snps:]
    backward(u[...], upper, lower, stats, out)
    out[:, 2 * half :] = lanes_of(total(u[...] * u[...]))


def advance(snps_all, sums, ridge, scalars, r, d, moved):
    rows = r.shape[1]
    norm, size = scalars[:, 0:1], scalars[:, 1:2]
    delta = ridge[:, 0:1]
    curve = sums[:, rows : rows + 1] / snps_all + delta * size
    step = norm / curve
    r_new = r[...] - step * (sums[:, :rows] / snps_all + delta * d[...])
    moved_new = step * d[...]
    if moved is not None:
        moved_new = moved[...] + moved_new
    return r_new, moved_new


def forward_kernel(snps_all, first, *refs):
    sums, ridge, scalars, r, d = refs[:5]
    moved = None if first else refs[5]
    upper, lower, stats, r_out, moved_out, out = refs[5 if first else 6 :]
    r_new, moved_out[...] = advance(snps_all, sums, ridge, scalars, r, d, moved)
    r_out[...] = r_new
    snps = upper.shape[1]
    forward(r_new, upper, lower, stats, out)
    out[:, snps:] = lanes_of(total(r_new * r_new), total(r_new * d[...]))


def backward_kernel(sums, u, r, d, scalars, upper, lower, stats, u_out, d_out, scalars_out, out):
    snps, half = upper.shape
    norm, size = scalars[:, 0:1], scalars[:, 1:2]
    norm_next, cross = sums[:, snps : snps + 1], sums[:, snps + 1 : snps + 2]
    ratio = norm_next / norm
    u_new = sums[:, :snps] + ratio * u[...]
    u_out[...] = u_new
    d_out[...] = r[...] + ratio * d[...]
    scalars_out[...] = lanes_of(norm_next, norm_next + 2.0 * ratio * cross + ratio * ratio * size)
    backward(u_new, upper, lower, stats, out)
    out[:, 2 * half :] = lanes_of(total(u_new * u_new))


def last_kernel(snps_all, sums, ridge, scalars, r, d, moved, r_out, moved_out, norm):
    r_new, moved_out[...] = advance(snps_all, sums, ridge, scalars, r, d, moved)
    r_out[...] = r_new
    norm[...] = lanes_of(total(r_new * r_new))


def own_kernel(r, d, moved, solution, s_out, r_out, d_out, r_keep):
    rows, own = r.shape[1], solution.shape[1]
    back = rows - (lax.axis_index("z") * lax.axis_size("x") + lax.axis_index("x")) * own
    s_out[...] = solution[...] + pltpu.roll(moved[...], back, 1)[:, :own]
    mine = pltpu.roll(r[...], back, 1)[:, :own]
    r_out[...] = mine
    r_keep[...] = mine
    d_out[...] = pltpu.roll(d[...], back, 1)[:, :own]


def call(kernel, outs, *args, name, dtypes=None, flops=0):
    spec = pl.BlockSpec(memory_space=pltpu.VMEM)
    return pl.pallas_call(
        kernel,
        out_shape=[jax.ShapeDtypeStruct(s, t) for s, t in zip(outs, dtypes or [F32] * len(outs))],
        in_specs=[spec] * len(args),
        out_specs=[spec] * len(outs),
        compiler_params=pltpu.CompilerParams(vmem_limit_bytes=VMEM_BYTES),
        cost_estimate=pl.CostEstimate(flops=flops, bytes_accessed=2**20, transcendentals=0),
        name=name,
    )(*args)


def swap_cores(value):
    return lax.ppermute(value, "c", [(0, 1), (1, 0)])


def swap_across(value, axis, k):
    names = ("y", "c") if axis == "y" else ("c", axis)
    size, chips = 2 * lax.axis_size(axis), lax.axis_size(axis)
    if axis == "y":
        pairs = [(i, i ^ (2 * k + 1)) for i in range(size)]
    else:
        pairs = [(i, i ^ (chips + k)) for i in range(size)]
    return lax.ppermute(value, names, pairs)


def crossed(value, axis):
    one, three, two = [swap_across(value, axis, k) for k in (1, 3, 2)]
    return [swap_cores(value), one, two, three]


def sum_crossed(value, axis):
    zero, one, two, three = crossed(value, axis)
    return (zero + one) + (three + two)


def local(genotypes, allele_counts, ridge, solution, residual, direction):
    rows, snps = genotypes.shape
    k, own = solution.shape
    samples_all = rows * lax.axis_size("y") * lax.axis_size("c")
    snps_all = snps * lax.axis_size("z") * lax.axis_size("x")
    ridge = jnp.broadcast_to(ridge[:, None], (ridge.shape[0], LANES))
    flops = 2 * 16 * rows * snps
    full, short = (k, rows + LANES), (k, snps + LANES)
    vec, row, col, mine = (k, rows), (k, snps), (k, LANES), (k, own)

    half = rows // 2
    steps = half // STEP_ROWS
    genotypes = pltpu.with_memory_space_constraint(genotypes, pltpu.HBM)

    def converted(part):
        return pl.pallas_call(
            functools.partial(convert_kernel, part),
            out_shape=jax.ShapeDtypeStruct((half, snps), BF16),
            in_specs=[pl.BlockSpec(memory_space=pltpu.HBM)],
            out_specs=pl.BlockSpec(memory_space=pltpu.VMEM),
            scratch_shapes=[
                pltpu.VMEM((steps, STEP_ROWS, snps), jnp.int32),
                pltpu.SemaphoreType.DMA((steps,)),
            ],
            compiler_params=pltpu.CompilerParams(vmem_limit_bytes=2 * VMEM_BYTES),
            cost_estimate=pl.CostEstimate(
                flops=half * snps, bytes_accessed=half * snps * 6, transcendentals=0
            ),
            name="convert",
        )(genotypes)

    (stats,) = call(
        functools.partial(stats_kernel, 2.0 * samples_all), ((8, snps),), allele_counts, name="stats"
    )
    both = jnp.concatenate([residual, direction], axis=0)
    upper = converted(0)
    quarter = jnp.concatenate(crossed(both, "x"), axis=1)
    quarter, upper = lax.optimization_barrier((quarter, upper))
    lower = converted(1)
    pieces = crossed(quarter, "z")
    *pieces, lower = lax.optimization_barrier((*pieces, lower))
    r, d, sums = call(
        first_forward_kernel, (vec, vec, short), *pieces, upper, lower, stats,
        name="first_forward", flops=flops,
    )
    def over_y(v):
        one, three, two = [swap_across(v, "y", k) for k in (1, 3, 2)]
        return (v + one) + (three + two)

    def over_samp(v):
        return over_y(v + swap_cores(v))

    def over_snp(v):
        return sum_crossed(sum_crossed(v, "x"), "z")

    moved = None
    for iteration in range(ITERS):
        if iteration == 0:
            sums = sums + swap_cores(sums)
            sums, *halves = lax.optimization_barrier((sums, upper, lower))
            turned = [
                call(turn_kernel, ((snps, half),), part, name="turn", dtypes=(BF16,), flops=2**30)[0]
                for part in halves
            ]
            sums = over_y(sums)
            u, scalars, sums = call(
                first_backward_kernel, (row, col, full), sums, *turned, stats,
                name="first_backward", flops=flops,
            )
        else:
            sums = over_samp(sums)
            u, d, scalars, sums = call(
                backward_kernel, (row, vec, col, full), sums, u, r, d, scalars, *turned, stats,
                name="backward", flops=flops,
            )
        sums = over_snp(sums)
        if iteration < ITERS - 1:
            state = (sums, ridge, scalars, r, d) + (() if moved is None else (moved,))
            r, moved, sums = call(
                functools.partial(forward_kernel, float(snps_all), moved is None),
                (vec, vec, short), *state, upper, lower, stats, name="forward", flops=flops,
            )
    r, moved, norm = call(
        functools.partial(last_kernel, float(snps_all)), (vec, vec, col),
        sums, ridge, scalars, r, d, moved, name="last",
    )
    solution, r_own, d, r = call(
        own_kernel, (mine, mine, mine, mine), r, d, moved, solution, name="own", flops=2**20
    )
    norm = over_samp(norm)
    return (solution, r_own, r + (norm[:, 0:1] / scalars[:, 0:1]) * d)


def solution(mesh):
    parts = jax.sharding.Mesh(mesh.devices.reshape(4, 2, 4, 4), ("y", "c", "z", "x"))
    vec = P(None, ("y", "c", "z", "x"))
    in_specs = (P(("y", "c"), ("z", "x")), P(("z", "x")), P(), vec, vec, vec)
    return jax.shard_map(
        local, mesh=parts, in_specs=in_specs, out_specs=(vec, vec, vec), check_vma=False
    )
```
